32 devices in a mesh: gx: 4 (over z), gy: 2 (over core), gz: 4 (over y, x).
Axes of the slice: x: 2, y: 2, z: 4, core: 2. Of those that a mesh axis runs over, the one named last changes fastest.
Arguments:
- traces: bfloat16 [2048, 32], P('gx'), may hold values from -6 to 6
- receiver_cell: int32 [2048], P('gx'), may hold values from 0 to 2047
- weight_class: int32 [2048], P('gx'), may hold values from 0 to 15
- weight_table: float32 [16], replicated, may hold values from 0.5 to 2
- obstacle_top: int32 [8, 64], P('gx', 'gy'), may hold values from 128 to 255
- obstacle_thick: int32 [8, 64], P('gx', 'gy'), may hold values from 0 to 128
- courant: float32 [16, 128, 512], P('gx', 'gy', 'gz'), may hold values from 0.06 to 0.25
- p_now: float32 [16, 128, 512], P('gx', 'gy', 'gz'), may hold values from -6 to 6
- p_prev: float32 [16, 128, 512], P('gx', 'gy', 'gz'), may hold values from -6 to 6
Outputs:
- wavefield: float32 [16, 128, 512], P('gx', 'gy', 'gz')
The draws below stay inside these ranges and needn't reach their ends.
All inputs are finite; a program needn't handle non-finite values.
Results may differ from the reference program's by a relative error of at most 0.0003.
Values may be sent and summed in bfloat16 or wider, within the bound.
A program may use at most 64 MiB of HBM per device.

```python
import math
import jax
import jax.numpy as jnp
from jax import lax

STEPS = 32
NW = 16
NX = 16
NY = 128
NZ = 512
NREC = 2048


def touch_ends(array, rng, smallest, high):
    dims = array.shape
    spot = [jax.random.randint(jax.random.fold_in(rng, axis), (), 0, dims[axis]) for axis in range(len(dims))]
    array = array.at[tuple(spot)].set(smallest)
    longest = dims.index(max(dims))
    spot[longest] = (spot[longest] + 1) % dims[longest]
    return array.at[tuple(spot)].set(high)


def steps_of(own_key, dims, split, low, high):
    factor_of = 1.0
    for axis_at, blocks in split:
        steps = jax.random.uniform(jax.random.fold_in(jax.random.fold_in(own_key, 6), axis_at), (blocks,), jnp.float32, low / len(split), high / len(split))
        factor_of = factor_of * jnp.repeat(jnp.exp(steps), dims[axis_at] // blocks).reshape((-1,) + (1,) * (len(dims) - 1 - axis_at))
    return factor_of


def scatter_about(key, dims, deviation, reach, shards=(), kind=jnp.bfloat16):
    array = deviation * jax.random.normal(key, dims, jnp.float32)
    if shards:
        array = array * steps_of(key, dims, shards, -0.22, 0.18)
    return jnp.clip(array, -reach, reach).astype(kind)


def setup_inputs(seed: int = 0) -> dict:
    streams_of = jax.random.split(jax.random.key(seed), 10)
    traces = scatter_about(streams_of[0], (NREC, STEPS), 1.0, 6.0, ((0, 4),))
    receiver_cell = touch_ends(jax.random.randint(streams_of[1], (NREC,), 0, NX * NY), jax.random.fold_in(streams_of[1], 1), 0, (NX * NY) - 1).astype(jnp.int32)
    weight_class = touch_ends(jax.random.randint(streams_of[2], (NREC,), 0, NW), jax.random.fold_in(streams_of[2], 1), 0, NW - 1).astype(jnp.int32)
    weight_table = jnp.clip(jnp.exp(jax.random.uniform(streams_of[3], (NW,), jnp.float32, math.log(0.5), math.log(2.0))), 0.5, 2.0)
    obstacle_top = touch_ends(jax.random.randint(streams_of[4], (NX // 2, NY // 2), NZ // 4, NZ // 2), jax.random.fold_in(streams_of[4], 1), NZ // 4, (NZ // 2) - 1).astype(jnp.int32)
    obstacle_thick = touch_ends(jax.random.randint(streams_of[5], (NX // 2, NY // 2), 0, NZ // 4 + 1), jax.random.fold_in(streams_of[5], 1), 0, (NZ // 4 + 1) - 1).astype(jnp.int32)
    courant = jnp.clip(jnp.exp(math.log(0.25) - 1.4271164 * jax.random.uniform(streams_of[6], (NX, NY, NZ), jnp.float32) ** steps_of(streams_of[6], (NX, NY, NZ), ((0, 4), (1, 2), (2, 4)), -0.2, 0.2)), 0.06, 0.25)
    p_now = scatter_about(streams_of[7], (NX, NY, NZ), 1.0, 6.0, ((0, 4), (1, 2), (2, 4)), jnp.float32)
    p_prev = scatter_about(streams_of[8], (NX, NY, NZ), 1.0, 6.0, ((0, 4), (1, 2), (2, 4)), jnp.float32)
    return {"traces": traces, "receiver_cell": receiver_cell, "weight_class": weight_class, "weight_table": weight_table, "obstacle_top": obstacle_top, "obstacle_thick": obstacle_thick, "courant": courant, "p_now": p_now, "p_prev": p_prev}


def laplace_zero(wavefield):
    padded = jnp.pad(wavefield, 1)
    beside_all = padded[2:, 1:-1, 1:-1] + padded[:-2, 1:-1, 1:-1]
    beside_all = beside_all + padded[1:-1, 2:, 1:-1] + padded[1:-1, :-2, 1:-1]
    beside_all = beside_all + padded[1:-1, 1:-1, 2:] + padded[1:-1, 1:-1, :-2]
    return beside_all - 6.0 * wavefield


def reference(traces, receiver_cell, weight_class, weight_table, obstacle_top, obstacle_thick, courant, p_now, p_prev):
    weights = weight_table[weight_class]
    contrib = weights[:, None] * traces.astype(jnp.float32)
    sources = jax.ops.segment_sum(contrib, receiver_cell, num_segments=NX * NY).reshape(NX, NY, STEPS)
    roof = jnp.repeat(jnp.repeat(obstacle_top, 2, axis=0), 2, axis=1)[:, :, None]
    thickness = jnp.repeat(jnp.repeat(obstacle_thick, 2, axis=0), 2, axis=1)[:, :, None]
    depth_cells = jnp.arange(NZ, dtype=jnp.int32)[None, None, :]
    solid = (depth_cells >= roof) & (depth_cells < roof + thickness)
    living = jnp.where(solid, 0.0, 1.0).astype(jnp.float32)
    surface = (jnp.arange(NZ, dtype=jnp.int32) == 0).astype(jnp.float32)

    def advance(counter, carried):
        current, previous = carried
        source_plane = lax.dynamic_index_in_dim(sources, STEPS - 1 - counter, 2, keepdims=False)
        updated = 2.0 * current - previous + courant * laplace_zero(current) + source_plane[:, :, None] * surface
        return (living * updated, current)

    current, previous = lax.fori_loop(0, STEPS, advance, (p_now, p_prev))
    return current
```

```python
import functools

import jax
import jax.numpy as jnp
from jax import lax
from jax.experimental import pallas as pl
from jax.experimental.pallas import tpu as pltpu
from jax.sharding import PartitionSpec as P

MESH = pl.DeviceIdType.MESH
AXES = ("gx", "gy", "gz")


def kernel(
    counts,
    grid_y,
    steps,
    trace_ref,
    tag_ref,
    table_ref,
    top_ref,
    thick_ref,
    courant_ref,
    now_ref,
    before_ref,
    out_ref,
    field,
    ghost_x,
    ghost_y,
    ghost_z,
    send_y,
    send_z,
    living,
    sources,
    traces,
    tags,
    send_sem,
    recv_sem,
    gather_send,
    gather_recv,
):
    tx, ty, tz = courant_ref.shape
    rows = ty // 8
    me = [lax.axis_index(a) for a in AXES]
    has_lo = [me[a] > 0 for a in range(3)]
    has_hi = [me[a] < counts[a] - 1 for a in range(3)]
    lo_id = [{AXES[a]: jnp.maximum(me[a] - 1, 0)} for a in range(3)]
    hi_id = [{AXES[a]: jnp.minimum(me[a] + 1, counts[a] - 1)} for a in range(3)]

    def copy(direction, slot):
        axis, upper = direction // 2, direction % 2
        if axis == 0:
            src = field.at[slot, tx - 1 if upper else 0]
            dst = ghost_x.at[slot, direction % 2]
        elif axis == 1:
            src = send_y.at[slot, upper]
            dst = ghost_y.at[slot, upper]
        else:
            src = send_z.at[slot, upper]
            dst = ghost_z.at[slot, upper]
        return pltpu.make_async_remote_copy(
            src_ref=src,
            dst_ref=dst,
            send_sem=send_sem.at[direction, slot],
            recv_sem=recv_sem.at[direction, slot],
            device_id=(hi_id if upper else lo_id)[axis],
            device_id_type=MESH,
        )

    def target(direction):
        return (has_hi if direction % 2 else has_lo)[direction // 2]

    def origin(direction):
        return (has_lo if direction % 2 else has_hi)[direction // 2]

    def start(direction, slot, also=None):
        cond = target(direction) if also is None else target(direction) & also

        @pl.when(cond)
        def _():
            copy(direction, slot).start()

    def wait_recv(direction, slot):
        @pl.when(origin(direction))
        def _():
            copy(direction, slot).wait_recv()

    def wait_send(direction, slot):
        @pl.when(target(direction))
        def _():
            copy(direction, slot).wait_send()

    ghost_x[...] = jnp.zeros_like(ghost_x)
    ghost_y[...] = jnp.zeros_like(ghost_y)
    ghost_z[...] = jnp.zeros_like(ghost_z)
    field[0] = now_ref[...]
    field[1] = before_ref[...]

    barrier = pltpu.get_barrier_semaphore()
    for d in range(1, counts[0]):
        pl.semaphore_signal(
            barrier,
            inc=1,
            device_id={"gx": lax.rem(me[0] + d, counts[0])},
            device_id_type=MESH,
        )
    for axis in (1, 2):

        @pl.when(has_lo[axis])
        def _():
            pl.semaphore_signal(barrier, inc=1, device_id=lo_id[axis], device_id_type=MESH)

        @pl.when(has_hi[axis])
        def _():
            pl.semaphore_signal(barrier, inc=1, device_id=hi_id[axis], device_id_type=MESH)

    greeted = counts[0] - 1
    for axis in (1, 2):
        greeted = greeted + has_lo[axis].astype(jnp.int32) + has_hi[axis].astype(jnp.int32)

    lane = lax.broadcasted_iota(jnp.int32, (8, tz), 1)

    def pack_z(slot):
        low = jnp.zeros((8, tz), jnp.float32)
        high = jnp.zeros((8, tz), jnp.float32)
        for x in range(tx):
            for b in range(rows):
                j = x * rows + b
                part = field[slot, x, b * 8 : b * 8 + 8, :]
                low = jnp.where(lane == j, pltpu.roll(part, j, 1) if j else part, low)
                high = jnp.where(lane == j, pltpu.roll(part, j + 1, 1), high)
        send_z[slot, 0] = low
        send_z[slot, 1] = high

    def pack_y(slot):
        for x in range(tx):
            send_y[slot, 0, x : x + 1, :] = field[slot, x, 0:1, :]
            send_y[slot, 1, x : x + 1, :] = field[slot, x, ty - 1 : ty, :]

    pack_y(0)
    pack_z(0)
    pl.semaphore_wait(barrier, greeted)
    for direction in range(6):
        start(direction, 0)

    def gather(d):
        there = {"gx": lax.rem(me[0] + d, counts[0])}
        pair = []
        for k, (src, dst) in enumerate(((trace_ref, traces), (tag_ref, tags))):
            pair.append(
                pltpu.make_async_remote_copy(
                    src_ref=src,
                    dst_ref=dst.at[d - 1],
                    send_sem=gather_send.at[d - 1, k],
                    recv_sem=gather_recv.at[d - 1, k],
                    device_id=there,
                    device_id_type=MESH,
                )
            )
        return pair

    for d in range(1, counts[0]):
        for c in gather(d):
            c.start()

    half_y = ty // 2
    pick = lax.broadcasted_iota(jnp.int32, (ty, half_y), 0) // 2 == lax.broadcasted_iota(
        jnp.int32, (ty, half_y), 1
    )
    depth = (me[2] * tz + lax.broadcasted_iota(jnp.int32, (ty, tz), 1)).astype(jnp.float32)
    for xb in range(tx // 2):
        top_row = top_ref[xb : xb + 1, :].astype(jnp.float32)
        thick_row = thick_ref[xb : xb + 1, :].astype(jnp.float32)
        top = jnp.sum(jnp.where(pick, top_row, 0.0), axis=1, keepdims=True)
        end = top + jnp.sum(jnp.where(pick, thick_row, 0.0), axis=1, keepdims=True)
        alive = jnp.where((depth >= top) & (depth < end), 0.0, 1.0)
        living[2 * xb] = alive
        living[2 * xb + 1] = alive

    cells = tx * ty
    row = lax.broadcasted_iota(jnp.int32, (cells, tag_ref.shape[1]), 0)
    surface = (me[2] == 0).astype(jnp.float32)

    def receivers(tag, trace):
        cell = tag[0:1, :]
        kind = tag[1:2, :]
        weight = jnp.zeros(kind.shape, jnp.float32)
        for c in range(table_ref.shape[0]):
            weight = jnp.where(kind == c, table_ref[c], weight)
        x = cell // grid_y - me[0] * tx
        y = cell % grid_y - me[1] * ty
        inside = (x >= 0) & (x < tx) & (y >= 0) & (y < ty)
        seg = jnp.where(inside, x * ty + y, -1)
        hit = row == seg
        total = None
        for _ in range(3):
            piece = weight.astype(jnp.bfloat16).astype(jnp.float32)
            weight = weight - piece
            spread = jnp.where(hit, piece, 0.0).astype(jnp.bfloat16)
            term = lax.dot_general(
                spread, trace, (((1,), (1,)), ((), ())), preferred_element_type=jnp.float32
            )
            total = term if total is None else total + term
        return total

    total = receivers(tag_ref[...], trace_ref[...])
    for d in range(1, counts[0]):
        for c in gather(d):
            c.wait()
        total = total + receivers(tags[d - 1], traces[d - 1])
    total = total * surface
    sources[...] = jnp.zeros_like(sources)
    for x in range(tx):
        sources[x, :, 0:steps] = total[x * ty : (x + 1) * ty]

    wide_lane = lax.broadcasted_iota(jnp.int32, (ty, tz), 1)
    wide_row = lax.broadcasted_iota(jnp.int32, (ty, tz), 0)

    def step(n, slot):
        new = 1 - slot
        more = n < steps - 1
        for direction in (2, 3, 4, 5):
            wait_recv(direction, slot)
        z_low = ghost_z[slot, 1]
        z_high = ghost_z[slot, 0]

        def plane(x, below, above):
            c = field[slot, x]
            y_low = jnp.where(wide_row == 0, ghost_y[slot, 1, x : x + 1, :], pltpu.roll(c, 1, 0))
            y_high = jnp.where(
                wide_row == ty - 1, ghost_y[slot, 0, x : x + 1, :], pltpu.roll(c, ty - 1, 0)
            )
            low_parts, high_parts = [], []
            for b in range(rows):
                j = x * rows + b
                low_parts.append(pltpu.roll(z_low, (tz - j) % tz, 1) if j else z_low)
                high_parts.append(pltpu.roll(z_high, tz - 1 - j, 1))
            left = jnp.where(
                wide_lane == 0, jnp.concatenate(low_parts, axis=0), pltpu.roll(c, 1, 1)
            )
            right = jnp.where(
                wide_lane == tz - 1, jnp.concatenate(high_parts, axis=0), pltpu.roll(c, tz - 1, 1)
            )
            laplace = above + below + y_high + y_low + right + left - 6.0 * c
            source = pltpu.roll(sources[x], lax.rem(n + 1 - steps + tz, tz), 1)
            source = jnp.where(wide_lane == 0, source, 0.0)
            updated = 2.0 * c - field[new, x] + courant_ref[x] * laplace + source
            field[new, x] = living[x] * updated

        for x in range(1, tx - 1):
            plane(x, field[slot, x - 1], field[slot, x + 1])
        wait_recv(1, slot)
        plane(0, ghost_x[slot, 1], field[slot, 1])
        start(0, new, more)
        wait_recv(0, slot)
        plane(tx - 1, field[slot, tx - 2], ghost_x[slot, 0])
        start(1, new, more)
        pack_y(new)
        start(2, new, more)
        start(3, new, more)
        pack_z(new)
        start(4, new, more)
        start(5, new, more)
        for direction in range(6):
            wait_send(direction, slot)

    def double_step(k, carry):
        step(2 * k, 0)
        step(2 * k + 1, 1)
        return carry

    lax.fori_loop(0, steps // 2, double_step, 0)
    out_ref[...] = field[0]


def local(counts, traces, receiver_cell, weight_class, weight_table, top, thick, courant, now, before):
    tx, ty, tz = courant.shape
    count, steps = traces.shape
    tag = jnp.stack([receiver_cell, weight_class])
    others = max(counts[0] - 1, 1)
    vmem = pl.BlockSpec(memory_space=pltpu.VMEM)
    smem = pl.BlockSpec(memory_space=pltpu.SMEM)
    return pl.pallas_call(
        functools.partial(kernel, counts, ty * counts[1], steps),
        out_shape=jax.ShapeDtypeStruct((tx, ty, tz), jnp.float32),
        in_specs=[vmem, vmem, smem, vmem, vmem, vmem, vmem, vmem],
        out_specs=vmem,
        scratch_shapes=[
            pltpu.VMEM((2, tx, ty, tz), jnp.float32),
            pltpu.VMEM((2, 2, ty, tz), jnp.float32),
            pltpu.VMEM((2, 2, tx, tz), jnp.float32),
            pltpu.VMEM((2, 2, 8, tz), jnp.float32),
            pltpu.VMEM((2, 2, tx, tz), jnp.float32),
            pltpu.VMEM((2, 2, 8, tz), jnp.float32),
            pltpu.VMEM((tx, ty, tz), jnp.float32),
            pltpu.VMEM((tx, ty, tz), jnp.float32),
            pltpu.VMEM((others, steps, count), jnp.bfloat16),
            pltpu.VMEM((others, 2, count), jnp.int32),
            pltpu.SemaphoreType.DMA((6, 2)),
            pltpu.SemaphoreType.DMA((6, 2)),
            pltpu.SemaphoreType.DMA((others, 2)),
            pltpu.SemaphoreType.DMA((others, 2)),
        ],
        compiler_params=pltpu.CompilerParams(
            collective_id=0, has_side_effects=True, vmem_limit_bytes=32 * 1024 * 1024
        ),
    )(traces.T, tag, weight_table, top, thick, courant, now, before)


def solution(mesh):
    counts = tuple(mesh.shape[a] for a in AXES)
    tile = P("gx", "gy", "gz")
    columns = P("gx", "gy")
    placed = (P("gx", None), P("gx"), P("gx"), P(), columns, columns, tile, tile, tile)
    return jax.shard_map(
        functools.partial(local, counts), mesh=mesh, in_specs=placed, out_specs=tile, check_vma=False
    )
```

```python
import functools

import jax
import jax.numpy as jnp
from jax import lax
from jax.experimental import pallas as pl
from jax.experimental.pallas import tpu as pltpu
from jax.sharding import PartitionSpec as P

MESH = pl.DeviceIdType.MESH
AXES = ("gx", "gy", "gz")


def kernel(
    counts,
    grid_y,
    steps,
    trace_ref,
    tag_ref,
    table_ref,
    top_ref,
    thick_ref,
    courant_ref,
    now_ref,
    before_ref,
    out_ref,
    field,
    ghost_x,
    ghost_y,
    ghost_z,
    send_y,
    send_z,
    living,
    sources,
    traces,
    tags,
    send_sem,
    recv_sem,
    gather_send,
    gather_recv,
):
    tx, ty, tz = courant_ref.shape
    rows = ty // 8
    me = [lax.axis_index(a) for a in AXES]
    has_lo = [me[a] > 0 for a in range(3)]
    has_hi = [me[a] < counts[a] - 1 for a in range(3)]
    lo_id = [{AXES[a]: jnp.maximum(me[a] - 1, 0)} for a in range(3)]
    hi_id = [{AXES[a]: jnp.minimum(me[a] + 1, counts[a] - 1)} for a in range(3)]

    def copy(direction, slot):
        axis, upper = direction // 2, direction % 2
        if axis == 0:
            src = field.at[slot, tx - 1 if upper else 0]
            dst = ghost_x.at[slot, direction % 2]
        elif axis == 1:
            src = send_y.at[slot, upper]
            dst = ghost_y.at[slot, upper]
        else:
            src = send_z.at[slot, upper]
            dst = ghost_z.at[slot, upper]
        return pltpu.make_async_remote_copy(
            src_ref=src,
            dst_ref=dst,
            send_sem=send_sem.at[direction, slot],
            recv_sem=recv_sem.at[direction, slot],
            device_id=(hi_id if upper else lo_id)[axis],
            device_id_type=MESH,
        )

    def target(direction):
        return (has_hi if direction % 2 else has_lo)[direction // 2]

    def origin(direction):
        return (has_lo if direction % 2 else has_hi)[direction // 2]

    def start(direction, slot, also=None):
        cond = target(direction) if also is None else target(direction) & also

        @pl.when(cond)
        def _():
            copy(direction, slot).start()

    def wait_recv(direction, slot):
        @pl.when(origin(direction))
        def _():
            copy(direction, slot).wait_recv()

    def wait_send(direction, slot):
        @pl.when(target(direction))
        def _():
            copy(direction, slot).wait_send()

    ghost_x[...] = jnp.zeros_like(ghost_x)
    ghost_y[...] = jnp.zeros_like(ghost_y)
    ghost_z[...] = jnp.zeros_like(ghost_z)
    field[0] = now_ref[...]
    field[1] = before_ref[...]

    barrier = pltpu.get_barrier_semaphore()
    for d in range(1, counts[0]):
        pl.semaphore_signal(
            barrier,
            inc=1,
            device_id={"gx": lax.rem(me[0] + d, counts[0])},
            device_id_type=MESH,
        )
    for axis in (1, 2):

        @pl.when(has_lo[axis])
        def _():
            pl.semaphore_signal(barrier, inc=1, device_id=lo_id[axis], device_id_type=MESH)

        @pl.when(has_hi[axis])
        def _():
            pl.semaphore_signal(barrier, inc=1, device_id=hi_id[axis], device_id_type=MESH)

    greeted = counts[0] - 1
    for axis in (1, 2):
        greeted = greeted + has_lo[axis].astype(jnp.int32) + has_hi[axis].astype(jnp.int32)

    lane = lax.broadcasted_iota(jnp.int32, (8, tz), 1)

    def pack_z(slot):
        low = jnp.zeros((8, tz), jnp.float32)
        high = jnp.zeros((8, tz), jnp.float32)
        for x in range(tx):
            for b in range(rows):
                j = x * rows + b
                part = field[slot, x, b * 8 : b * 8 + 8, :]
                low = jnp.where(lane == j, pltpu.roll(part, j, 1) if j else part, low)
                high = jnp.where(lane == j, pltpu.roll(part, j + 1, 1), high)
        send_z[slot, 0] = low
        send_z[slot, 1] = high

    def pack_y(slot):
        for x in range(tx):
            send_y[slot, 0, x : x + 1, :] = field[slot, x, 0:1, :]
            send_y[slot, 1, x : x + 1, :] = field[slot, x, ty - 1 : ty, :]

    pack_y(0)
    pack_z(0)
    pl.semaphore_wait(barrier, greeted)
    for direction in range(6):
        start(direction, 0)

    def gather(d):
        there = {"gx": lax.rem(me[0] + d, counts[0])}
        pair = []
        for k, (src, dst) in enumerate(((trace_ref, traces), (tag_ref, tags))):
            pair.append(
                pltpu.make_async_remote_copy(
                    src_ref=src,
                    dst_ref=dst.at[d - 1],
                    send_sem=gather_send.at[d - 1, k],
                    recv_sem=gather_recv.at[d - 1, k],
                    device_id=there,
                    device_id_type=MESH,
                )
            )
        return pair

    for d in range(1, counts[0]):
        for c in gather(d):
            c.start()

    half_y = ty // 2
    pick = lax.broadcasted_iota(jnp.int32, (ty, half_y), 0) // 2 == lax.broadcasted_iota(
        jnp.int32, (ty, half_y), 1
    )
    depth = (me[2] * tz + lax.broadcasted_iota(jnp.int32, (ty, tz), 1)).astype(jnp.float32)
    for xb in range(tx // 2):
        top_row = top_ref[xb : xb + 1, :].astype(jnp.float32)
        thick_row = thick_ref[xb : xb + 1, :].astype(jnp.float32)
        top = jnp.sum(jnp.where(pick, top_row, 0.0), axis=1, keepdims=True)
        end = top + jnp.sum(jnp.where(pick, thick_row, 0.0), axis=1, keepdims=True)
        alive = jnp.where((depth >= top) & (depth < end), 0.0, 1.0)
        living[2 * xb] = alive
        living[2 * xb + 1] = alive

    cells = tx * ty
    row = lax.broadcasted_iota(jnp.int32, (cells, tag_ref.shape[1]), 0)
    surface = (me[2] == 0).astype(jnp.float32)

    def receivers(tag, trace):
        cell = tag[0:1, :]
        kind = tag[1:2, :]
        weight = jnp.zeros(kind.shape, jnp.float32)
        for c in range(table_ref.shape[0]):
            weight = jnp.where(kind == c, table_ref[c], weight)
        x = cell // grid_y - me[0] * tx
        y = cell % grid_y - me[1] * ty
        inside = (x >= 0) & (x < tx) & (y >= 0) & (y < ty)
        seg = jnp.where(inside, x * ty + y, -1)
        hit = row == seg
        total = None
        for _ in range(3):
            piece = weight.astype(jnp.bfloat16).astype(jnp.float32)
            weight = weight - piece
            spread = jnp.where(hit, piece, 0.0).astype(jnp.bfloat16)
            term = lax.dot_general(
                spread, trace, (((1,), (1,)), ((), ())), preferred_element_type=jnp.float32
            )
            total = term if total is None else total + term
        return total

    total = receivers(tag_ref[...], trace_ref[...])
    for d in range(1, counts[0]):
        for c in gather(d):
            c.wait()
        total = total + receivers(tags[d - 1], traces[d - 1])
    total = total * surface
    sources[...] = jnp.zeros_like(sources)
    for x in range(tx):
        sources[x, :, 0:steps] = total[x * ty : (x + 1) * ty]

    wide_lane = lax.broadcasted_iota(jnp.int32, (ty, tz), 1)
    wide_row = lax.broadcasted_iota(jnp.int32, (ty, tz), 0)

    def step(n, slot):
        new = 1 - slot
        more = n < steps - 1
        for direction in (2, 3, 4, 5):
            wait_recv(direction, slot)
        z_low = ghost_z[slot, 1]
        z_high = ghost_z[slot, 0]

        def plane(x, below, above):
            c = field[slot, x]
            y_low = jnp.where(wide_row == 0, ghost_y[slot, 1, x : x + 1, :], pltpu.roll(c, 1, 0))
            y_high = jnp.where(
                wide_row == ty - 1, ghost_y[slot, 0, x : x + 1, :], pltpu.roll(c, ty - 1, 0)
            )
            low_parts, high_parts = [], []
            for b in range(rows):
                j = x * rows + b
                low_parts.append(pltpu.roll(z_low, (tz - j) % tz, 1) if j else z_low)
                high_parts.append(pltpu.roll(z_high, tz - 1 - j, 1))
            left = jnp.where(
                wide_lane == 0, jnp.concatenate(low_parts, axis=0), pltpu.roll(c, 1, 1)
            )
            right = jnp.where(
                wide_lane == tz - 1, jnp.concatenate(high_parts, axis=0), pltpu.roll(c, tz - 1, 1)
            )
            laplace = above + below + y_high + y_low + right + left - 6.0 * c
            source = pltpu.roll(sources[x], lax.rem(n + 1 - steps + tz, tz), 1)
            source = jnp.where(wide_lane == 0, source, 0.0)
            updated = 2.0 * c - field[new, x] + courant_ref[x] * laplace + source
            field[new, x] = living[x] * updated

        for x in range(1, tx - 1):
            plane(x, field[slot, x - 1], field[slot, x + 1])
        wait_recv(1, slot)
        plane(0, ghost_x[slot, 1], field[slot, 1])
        start(0, new, more)
        wait_recv(0, slot)
        plane(tx - 1, field[slot, tx - 2], ghost_x[slot, 0])
        start(1, new, more)
        pack_y(new)
        start(2, new, more)
        start(3, new, more)
        pack_z(new)
        start(4, new, more)
        start(5, new, more)
        for direction in range(6):
            wait_send(direction, slot)

    def double_step(k, carry):
        step(2 * k, 0)
        step(2 * k + 1, 1)
        return carry

    lax.fori_loop(0, steps // 2, double_step, 0)
    out_ref[...] = field[0]

DEEP = 8


def slab_kernel(
    counts,
    grid_y,
    steps,
    trace_ref,
    tag_ref,
    table_ref,
    top_ref,
    thick_ref,
    courant_ref,
    now_ref,
    before_ref,
    out_ref,
    field,
    mine,
    land_y,
    land_z,
    send_z,
    sources,
    traces,
    tags,
    result,
    halo_send,
    halo_recv,
    swap_send,
    swap_recv,
    gather_send,
    gather_recv,
    back_send,
    back_recv,
):
    tx, ty, tz = courant_ref.shape
    nx = counts[0]
    full_x = tx * nx
    own = ty // nx
    rows = own + 2 * DEEP
    gx, gy, gz = [lax.axis_index(a) for a in AXES]

    def rank_of(x, y):
        return jnp.where(y % 2 == 0, x, nx - 1 - x)

    place = gy * nx + rank_of(gx, gy)
    slabs = nx * counts[1]

    hops = [(dy, dz) for dy in (-1, 0, 1) for dz in (-1, 0, 1) if dy or dz]

    def exists(dy, dz):
        s, z = place + dy, gz + dz
        return (s >= 0) & (s < slabs) & (z >= 0) & (z < counts[2])

    def device(dy, dz):
        s = jnp.clip(place + dy, 0, slabs - 1)
        z = jnp.clip(gz + dz, 0, counts[2] - 1)
        y = s // nx
        return (rank_of(s % nx, y), y, z)

    def other(d):
        return lax.rem(gx + d, nx)

    field[...] = jnp.zeros_like(field)
    land_y[...] = jnp.zeros_like(land_y)
    land_z[...] = jnp.zeros_like(land_z)

    barrier = pltpu.get_barrier_semaphore()
    for d in range(1, nx):
        pl.semaphore_signal(barrier, inc=1, device_id=(other(d), gy, gz), device_id_type=MESH)
    greeted = nx - 1
    for hop in hops:
        greeted = greeted + exists(*hop).astype(jnp.int32)

        @pl.when(exists(*hop))
        def _():
            pl.semaphore_signal(barrier, inc=1, device_id=device(*hop), device_id_type=MESH)

    mine[0] = before_ref[...]
    mine[1] = now_ref[...]
    half_y = ty // 2
    pick = lax.broadcasted_iota(jnp.int32, (ty, half_y), 0) // 2 == lax.broadcasted_iota(
        jnp.int32, (ty, half_y), 1
    )
    depth = (gz * tz + lax.broadcasted_iota(jnp.int32, (ty, tz), 1)).astype(jnp.float32)
    for xb in range(tx // 2):
        top_row = top_ref[xb : xb + 1, :].astype(jnp.float32)
        thick_row = thick_ref[xb : xb + 1, :].astype(jnp.float32)
        top = jnp.sum(jnp.where(pick, top_row, 0.0), axis=1, keepdims=True)
        end = top + jnp.sum(jnp.where(pick, thick_row, 0.0), axis=1, keepdims=True)
        solid = (depth >= top) & (depth < end)
        for x in (2 * xb, 2 * xb + 1):
            mine[2, x] = jnp.where(solid, 0.0, courant_ref[x])

    pl.semaphore_wait(barrier, greeted)

    def swap(d):
        first = pl.multiple_of(rank_of(other(d), gy) * own, 8)
        return pltpu.make_async_remote_copy(
            src_ref=mine.at[:, :, pl.ds(first, own), :],
            dst_ref=field.at[:, pl.ds(gx * tx, tx), pl.ds(DEEP, own), pl.ds(0, tz)],
            send_sem=swap_send.at[d - 1],
            recv_sem=swap_recv.at[d - 1],
            device_id=(other(d), gy, gz),
            device_id_type=MESH,
        )

    def gather(d):
        pair = []
        for k, (src, dst) in enumerate(((trace_ref, traces), (tag_ref, tags))):
            pair.append(
                pltpu.make_async_remote_copy(
                    src_ref=src,
                    dst_ref=dst.at[d - 1],
                    send_sem=gather_send.at[d - 1, k],
                    recv_sem=gather_recv.at[d - 1, k],
                    device_id=(other(d), gy, gz),
                    device_id_type=MESH,
                )
            )
        return pair

    for d in range(1, nx):
        swap(d).start()
    for d in range(1, nx):
        for c in gather(d):
            c.start()
    first = pl.multiple_of(rank_of(gx, gy) * own, 8)
    for x in range(tx):
        field[:, gx * tx + x, DEEP : DEEP + own, 0:tz] = mine[:, x, pl.ds(first, own), :]

    lane = lax.broadcasted_iota(jnp.int32, (own, tz), 1)
    tall_lane = lax.broadcasted_iota(jnp.int32, (rows, tz), 1)

    def halo(hop, slot, fields):
        dy, dz = hop
        k = hops.index(hop)
        if dz == 0:
            src = field.at[
                pl.ds(0, fields), :, pl.ds(DEEP if dy < 0 else own, DEEP), pl.ds(0, tz)
            ]
            dst = land_y.at[slot, 1 if dy < 0 else 0, pl.ds(0, fields)]
        else:
            from_row, to_row, size = {
                -1: (0, DEEP + own, DEEP),
                0: (0, DEEP, own),
                1: (own - DEEP, 0, DEEP),
            }[dy]
            src = send_z.at[1 if dz > 0 else 0, pl.ds(0, fields), pl.ds(from_row, size)]
            dst = land_z.at[slot, 1 if dz < 0 else 0, pl.ds(0, fields), pl.ds(to_row, size)]
        return pltpu.make_async_remote_copy(
            src_ref=src,
            dst_ref=dst,
            send_sem=halo_send.at[k, slot],
            recv_sem=halo_recv.at[k, slot],
            device_id=device(dy, dz),
            device_id_type=MESH,
        )

    def send_halos(slot, fields):
        for hop in hops:
            if hop[1] == 0:

                @pl.when(exists(*hop))
                def _():
                    halo(hop, slot, fields).start()

        for f in range(fields):
            low = jnp.zeros((own, tz), jnp.float32)
            high = jnp.zeros((own, tz), jnp.float32)
            for x in range(full_x):
                part = field[f, x, DEEP : DEEP + own, 0:tz]
                at = x * DEEP
                here = (lane >= at) & (lane < at + DEEP)
                low = jnp.where(here, pltpu.roll(part, at, 1) if at else part, low)
                turn = (at + DEEP) % tz
                high = jnp.where(here, pltpu.roll(part, turn, 1) if turn else part, high)
            send_z[0, f] = low
            send_z[1, f] = high
        for hop in hops:
            if hop[1] != 0:

                @pl.when(exists(*hop))
                def _():
                    halo(hop, slot, fields).start()

    def take_halos(slot, fields):
        for hop in hops:

            @pl.when(exists(-hop[0], -hop[1]))
            def _():
                halo(hop, slot, fields).wait_recv()

        for hop in hops:

            @pl.when(exists(*hop))
            def _():
                halo(hop, slot, fields).wait_send()

        for f in range(fields):
            from_low = land_z[slot, 0, f]
            from_high = land_z[slot, 1, f]
            for x in range(full_x):
                field[f, x, 0:DEEP, 0:tz] = land_y[slot, 0, f, x]
                field[f, x, DEEP + own : rows, 0:tz] = land_y[slot, 1, f, x]
                right = pltpu.roll(from_high, (tz - x * DEEP) % tz, 1) if x else from_high
                turn = (2 * tz - DEEP - x * DEEP) % tz
                left = pltpu.roll(from_low, turn, 1) if turn else from_low
                field[f, x, :, tz : 2 * tz] = jnp.where(
                    tall_lane < DEEP, right, jnp.where(tall_lane >= tz - DEEP, left, 0.0)
                )

    for d in range(1, nx):
        swap(d).wait()
    send_halos(0, 3)

    cells = full_x * rows
    row = lax.broadcasted_iota(jnp.int32, (cells, tag_ref.shape[1]), 0)
    surface = (gz == 0).astype(jnp.float32)

    def receivers(tag, trace):
        cell = tag[0:1, :]
        kind = tag[1:2, :]
        weight = jnp.zeros(kind.shape, jnp.float32)
        for c in range(table_ref.shape[0]):
            weight = jnp.where(kind == c, table_ref[c], weight)
        y = cell % grid_y - place * own + DEEP
        seg = jnp.where((y >= 0) & (y < rows), cell // grid_y * rows + y, -1)
        hit = jnp.where(row == seg, 1.0, 0.0).astype(jnp.bfloat16)
        left = weight * trace.astype(jnp.float32)
        total = None
        for _ in range(3):
            piece = left.astype(jnp.bfloat16)
            left = left - piece.astype(jnp.float32)
            term = lax.dot_general(
                hit, piece, (((1,), (1,)), ((), ())), preferred_element_type=jnp.float32
            )
            total = term if total is None else total + term
        return total

    total = receivers(tag_ref[...], trace_ref[...])
    for d in range(1, nx):
        for c in gather(d):
            c.wait()
        total = total + receivers(tags[d - 1], traces[d - 1])
    total = total * surface
    sources[...] = jnp.zeros_like(sources)
    for x in range(full_x):
        sources[x, :, 0:steps] = total[x * rows : (x + 1) * rows]

    wide = 2 * tz

    def step(n, current):
        new = 1 - current
        turn = lax.rem(n + 1 - steps + tz, tz)
        for x in range(full_x):
            c = field[current, x]
            around = pltpu.roll(c, 1, 0) + pltpu.roll(c, rows - 1, 0)
            around = around + (pltpu.roll(c, 1, 1) + pltpu.roll(c, wide - 1, 1))
            if x > 0:
                around = around + field[current, x - 1]
            if x < full_x - 1:
                around = around + field[current, x + 1]
            speed = field[2, x]
            source = jnp.where(tall_lane == 0, pltpu.roll(sources[x], turn, 1), 0.0)
            source = jnp.concatenate([source, jnp.zeros_like(source)], axis=1)
            updated = 2.0 * c - field[new, x] + speed * (around - 6.0 * c) + source
            field[new, x] = jnp.where(speed > 0.0, updated, 0.0)

    def advance(r):
        def double_step(k, carry):
            step(r * DEEP + 2 * k, 1)
            step(r * DEEP + 2 * k + 1, 0)
            return carry

        lax.fori_loop(0, DEEP // 2, double_step, 0)

    take_halos(0, 3)
    advance(0)

    def round_of(r, carry):
        slot = r % 2
        send_halos(slot, 2)
        take_halos(slot, 2)
        advance(r)
        return carry

    lax.fori_loop(1, steps // DEEP, round_of, 0)

    def back(d):
        return pltpu.make_async_remote_copy(
            src_ref=field.at[1, pl.ds(other(d) * tx, tx), pl.ds(DEEP, own), pl.ds(0, tz)],
            dst_ref=result.at[:, pl.ds(first, own), :],
            send_sem=back_send.at[d - 1],
            recv_sem=back_recv.at[d - 1],
            device_id=(other(d), gy, gz),
            device_id_type=MESH,
        )

    for d in range(1, nx):
        back(d).start()
    for x in range(tx):
        result[x, pl.ds(first, own), :] = field[1, gx * tx + x, DEEP : DEEP + own, 0:tz]
    for d in range(1, nx):
        back(d).wait()
    out_ref[...] = result[...]


def slab_scratch(counts, tx, ty, tz, count, steps):
    nx = counts[0]
    own = ty // nx
    rows = own + 2 * DEEP
    full_x = tx * nx
    others = max(nx - 1, 1)
    sem = pltpu.SemaphoreType.DMA
    return [
        pltpu.VMEM((3, full_x, rows, 2 * tz), jnp.float32),
        pltpu.VMEM((3, tx, ty, tz), jnp.float32),
        pltpu.VMEM((2, 2, 3, full_x, DEEP, tz), jnp.float32),
        pltpu.VMEM((2, 2, 3, rows, tz), jnp.float32),
        pltpu.VMEM((2, 3, own, tz), jnp.float32),
        pltpu.VMEM((full_x, rows, tz), jnp.float32),
        pltpu.VMEM((others, steps, count), jnp.bfloat16),
        pltpu.VMEM((others, 2, count), jnp.int32),
        pltpu.VMEM((tx, ty, tz), jnp.float32),
        sem((8, 2)),
        sem((8, 2)),
        sem((others,)),
        sem((others,)),
        sem((others, 2)),
        sem((others, 2)),
        sem((others,)),
        sem((others,)),
    ]


def slabs_fit(counts, tx, ty, tz, steps):
    own = ty // counts[0]
    return (
        own * counts[0] == ty
        and own % DEEP == 0
        and tx * counts[0] * DEEP == tz
        and steps % DEEP == 0
        and steps <= tz
    )


def face_scratch(counts, tx, ty, tz, count, steps):
    others = max(counts[0] - 1, 1)
    return [
        pltpu.VMEM((2, tx, ty, tz), jnp.float32),
        pltpu.VMEM((2, 2, ty, tz), jnp.float32),
        pltpu.VMEM((2, 2, tx, tz), jnp.float32),
        pltpu.VMEM((2, 2, 8, tz), jnp.float32),
        pltpu.VMEM((2, 2, tx, tz), jnp.float32),
        pltpu.VMEM((2, 2, 8, tz), jnp.float32),
        pltpu.VMEM((tx, ty, tz), jnp.float32),
        pltpu.VMEM((tx, ty, tz), jnp.float32),
        pltpu.VMEM((others, steps, count), jnp.bfloat16),
        pltpu.VMEM((others, 2, count), jnp.int32),
        pltpu.SemaphoreType.DMA((6, 2)),
        pltpu.SemaphoreType.DMA((6, 2)),
        pltpu.SemaphoreType.DMA((others, 2)),
        pltpu.SemaphoreType.DMA((others, 2)),
    ]


def local(counts, traces, receiver_cell, weight_class, weight_table, top, thick, courant, now, before):
    tx, ty, tz = courant.shape
    count, steps = traces.shape
    tag = jnp.stack([receiver_cell, weight_class])
    vmem = pl.BlockSpec(memory_space=pltpu.VMEM)
    smem = pl.BlockSpec(memory_space=pltpu.SMEM)
    if slabs_fit(counts, tx, ty, tz, steps):
        body, number = slab_kernel, 1
        scratch = slab_scratch(counts, tx, ty, tz, count, steps)
    else:
        body, number = kernel, 0
        scratch = face_scratch(counts, tx, ty, tz, count, steps)
    return pl.pallas_call(
        functools.partial(body, counts, ty * counts[1], steps),
        out_shape=jax.ShapeDtypeStruct((tx, ty, tz), jnp.float32),
        in_specs=[vmem, vmem, smem, vmem, vmem, vmem, vmem, vmem],
        out_specs=vmem,
        scratch_shapes=scratch,
        compiler_params=pltpu.CompilerParams(
            collective_id=number, has_side_effects=True, vmem_limit_bytes=32 * 1024 * 1024
        ),
    )(traces.T, tag, weight_table, top, thick, courant, now, before)


def solution(mesh):
    counts = tuple(mesh.shape[a] for a in AXES)
    tile = P("gx", "gy", "gz")
    columns = P("gx", "gy")
    placed = (P("gx", None), P("gx"), P("gx"), P(), columns, columns, tile, tile, tile)
    return jax.shard_map(
        functools.partial(local, counts), mesh=mesh, in_specs=placed, out_specs=tile, check_vma=False
    )
```

```python
import functools

import jax
import jax.numpy as jnp
from jax import lax
from jax.experimental import pallas as pl
from jax.experimental.pallas import tpu as pltpu
from jax.sharding import PartitionSpec as P

MESH = pl.DeviceIdType.MESH
AXES = ("gx", "gy", "gz")


def kernel(
    counts,
    grid_y,
    steps,
    trace_ref,
    tag_ref,
    table_ref,
    top_ref,
    thick_ref,
    courant_ref,
    now_ref,
    before_ref,
    out_ref,
    field,
    ghost_x,
    ghost_y,
    ghost_z,
    send_y,
    send_z,
    living,
    sources,
    traces,
    tags,
    send_sem,
    recv_sem,
    gather_send,
    gather_recv,
):
    tx, ty, tz = courant_ref.shape
    rows = ty // 8
    me = [lax.axis_index(a) for a in AXES]
    has_lo = [me[a] > 0 for a in range(3)]
    has_hi = [me[a] < counts[a] - 1 for a in range(3)]
    lo_id = [{AXES[a]: jnp.maximum(me[a] - 1, 0)} for a in range(3)]
    hi_id = [{AXES[a]: jnp.minimum(me[a] + 1, counts[a] - 1)} for a in range(3)]

    def copy(direction, slot):
        axis, upper = direction // 2, direction % 2
        if axis == 0:
            src = field.at[slot, tx - 1 if upper else 0]
            dst = ghost_x.at[slot, direction % 2]
        elif axis == 1:
            src = send_y.at[slot, upper]
            dst = ghost_y.at[slot, upper]
        else:
            src = send_z.at[slot, upper]
            dst = ghost_z.at[slot, upper]
        return pltpu.make_async_remote_copy(
            src_ref=src,
            dst_ref=dst,
            send_sem=send_sem.at[direction, slot],
            recv_sem=recv_sem.at[direction, slot],
            device_id=(hi_id if upper else lo_id)[axis],
            device_id_type=MESH,
        )

    def target(direction):
        return (has_hi if direction % 2 else has_lo)[direction // 2]

    def origin(direction):
        return (has_lo if direction % 2 else has_hi)[direction // 2]

    def start(direction, slot, also=None):
        cond = target(direction) if also is None else target(direction) & also

        @pl.when(cond)
        def _():
            copy(direction, slot).start()

    def wait_recv(direction, slot):
        @pl.when(origin(direction))
        def _():
            copy(direction, slot).wait_recv()

    def wait_send(direction, slot):
        @pl.when(target(direction))
        def _():
            copy(direction, slot).wait_send()

    ghost_x[...] = jnp.zeros_like(ghost_x)
    ghost_y[...] = jnp.zeros_like(ghost_y)
    ghost_z[...] = jnp.zeros_like(ghost_z)
    field[0] = now_ref[...]
    field[1] = before_ref[...]

    barrier = pltpu.get_barrier_semaphore()
    for d in range(1, counts[0]):
        pl.semaphore_signal(
            barrier,
            inc=1,
            device_id={"gx": lax.rem(me[0] + d, counts[0])},
            device_id_type=MESH,
        )
    for axis in (1, 2):

        @pl.when(has_lo[axis])
        def _():
            pl.semaphore_signal(barrier, inc=1, device_id=lo_id[axis], device_id_type=MESH)

        @pl.when(has_hi[axis])
        def _():
            pl.semaphore_signal(barrier, inc=1, device_id=hi_id[axis], device_id_type=MESH)

    greeted = counts[0] - 1
    for axis in (1, 2):
        greeted = greeted + has_lo[axis].astype(jnp.int32) + has_hi[axis].astype(jnp.int32)

    lane = lax.broadcasted_iota(jnp.int32, (8, tz), 1)

    def pack_z(slot):
        low = jnp.zeros((8, tz), jnp.float32)
        high = jnp.zeros((8, tz), jnp.float32)
        for x in range(tx):
            for b in range(rows):
                j = x * rows + b
                part = field[slot, x, b * 8 : b * 8 + 8, :]
                low = jnp.where(lane == j, pltpu.roll(part, j, 1) if j else part, low)
                high = jnp.where(lane == j, pltpu.roll(part, j + 1, 1), high)
        send_z[slot, 0] = low
        send_z[slot, 1] = high

    def pack_y(slot):
        for x in range(tx):
            send_y[slot, 0, x : x + 1, :] = field[slot, x, 0:1, :]
            send_y[slot, 1, x : x + 1, :] = field[slot, x, ty - 1 : ty, :]

    pack_y(0)
    pack_z(0)
    pl.semaphore_wait(barrier, greeted)
    for direction in range(6):
        start(direction, 0)

    def gather(d):
        there = {"gx": lax.rem(me[0] + d, counts[0])}
        pair = []
        for k, (src, dst) in enumerate(((trace_ref, traces), (tag_ref, tags))):
            pair.append(
                pltpu.make_async_remote_copy(
                    src_ref=src,
                    dst_ref=dst.at[d - 1],
                    send_sem=gather_send.at[d - 1, k],
                    recv_sem=gather_recv.at[d - 1, k],
                    device_id=there,
                    device_id_type=MESH,
                )
            )
        return pair

    for d in range(1, counts[0]):
        for c in gather(d):
            c.start()

    half_y = ty // 2
    pick = lax.broadcasted_iota(jnp.int32, (ty, half_y), 0) // 2 == lax.broadcasted_iota(
        jnp.int32, (ty, half_y), 1
    )
    depth = (me[2] * tz + lax.broadcasted_iota(jnp.int32, (ty, tz), 1)).astype(jnp.float32)
    for xb in range(tx // 2):
        top_row = top_ref[xb : xb + 1, :].astype(jnp.float32)
        thick_row = thick_ref[xb : xb + 1, :].astype(jnp.float32)
        top = jnp.sum(jnp.where(pick, top_row, 0.0), axis=1, keepdims=True)
        end = top + jnp.sum(jnp.where(pick, thick_row, 0.0), axis=1, keepdims=True)
        alive = jnp.where((depth >= top) & (depth < end), 0.0, 1.0)
        living[2 * xb] = alive
        living[2 * xb + 1] = alive

    cells = tx * ty
    row = lax.broadcasted_iota(jnp.int32, (cells, tag_ref.shape[1]), 0)
    surface = (me[2] == 0).astype(jnp.float32)

    def receivers(tag, trace):
        cell = tag[0:1, :]
        kind = tag[1:2, :]
        weight = jnp.zeros(kind.shape, jnp.float32)
        for c in range(table_ref.shape[0]):
            weight = jnp.where(kind == c, table_ref[c], weight)
        x = cell // grid_y - me[0] * tx
        y = cell % grid_y - me[1] * ty
        inside = (x >= 0) & (x < tx) & (y >= 0) & (y < ty)
        seg = jnp.where(inside, x * ty + y, -1)
        hit = row == seg
        total = None
        for _ in range(3):
            piece = weight.astype(jnp.bfloat16).astype(jnp.float32)
            weight = weight - piece
            spread = jnp.where(hit, piece, 0.0).astype(jnp.bfloat16)
            term = lax.dot_general(
                spread, trace, (((1,), (1,)), ((), ())), preferred_element_type=jnp.float32
            )
            total = term if total is None else total + term
        return total

    total = receivers(tag_ref[...], trace_ref[...])
    for d in range(1, counts[0]):
        for c in gather(d):
            c.wait()
        total = total + receivers(tags[d - 1], traces[d - 1])
    total = total * surface
    sources[...] = jnp.zeros_like(sources)
    for x in range(tx):
        sources[x, :, 0:steps] = total[x * ty : (x + 1) * ty]

    wide_lane = lax.broadcasted_iota(jnp.int32, (ty, tz), 1)
    wide_row = lax.broadcasted_iota(jnp.int32, (ty, tz), 0)

    def step(n, slot):
        new = 1 - slot
        more = n < steps - 1
        for direction in (2, 3, 4, 5):
            wait_recv(direction, slot)
        z_low = ghost_z[slot, 1]
        z_high = ghost_z[slot, 0]

        def plane(x, below, above):
            c = field[slot, x]
            y_low = jnp.where(wide_row == 0, ghost_y[slot, 1, x : x + 1, :], pltpu.roll(c, 1, 0))
            y_high = jnp.where(
                wide_row == ty - 1, ghost_y[slot, 0, x : x + 1, :], pltpu.roll(c, ty - 1, 0)
            )
            low_parts, high_parts = [], []
            for b in range(rows):
                j = x * rows + b
                low_parts.append(pltpu.roll(z_low, (tz - j) % tz, 1) if j else z_low)
                high_parts.append(pltpu.roll(z_high, tz - 1 - j, 1))
            left = jnp.where(
                wide_lane == 0, jnp.concatenate(low_parts, axis=0), pltpu.roll(c, 1, 1)
            )
            right = jnp.where(
                wide_lane == tz - 1, jnp.concatenate(high_parts, axis=0), pltpu.roll(c, tz - 1, 1)
            )
            laplace = above + below + y_high + y_low + right + left - 6.0 * c
            source = pltpu.roll(sources[x], lax.rem(n + 1 - steps + tz, tz), 1)
            source = jnp.where(wide_lane == 0, source, 0.0)
            updated = 2.0 * c - field[new, x] + courant_ref[x] * laplace + source
            field[new, x] = living[x] * updated

        for x in range(1, tx - 1):
            plane(x, field[slot, x - 1], field[slot, x + 1])
        wait_recv(1, slot)
        plane(0, ghost_x[slot, 1], field[slot, 1])
        start(0, new, more)
        wait_recv(0, slot)
        plane(tx - 1, field[slot, tx - 2], ghost_x[slot, 0])
        start(1, new, more)
        pack_y(new)
        start(2, new, more)
        start(3, new, more)
        pack_z(new)
        start(4, new, more)
        start(5, new, more)
        for direction in range(6):
            wait_send(direction, slot)

    def double_step(k, carry):
        step(2 * k, 0)
        step(2 * k + 1, 1)
        return carry

    lax.fori_loop(0, steps // 2, double_step, 0)
    out_ref[...] = field[0]

DEEP = 8


def slab_kernel(
    counts,
    grid_y,
    steps,
    trace_ref,
    tag_ref,
    table_ref,
    top_ref,
    thick_ref,
    courant_ref,
    now_ref,
    before_ref,
    out_ref,
    field,
    mine,
    land_y,
    land_z,
    send_z,
    sources,
    traces,
    tags,
    result,
    halo_send,
    halo_recv,
    swap_send,
    swap_recv,
    gather_send,
    gather_recv,
    back_send,
    back_recv,
    tops,
    thicks,
    fetch_sem,
):
    tx, ty, tz = courant_ref.shape
    nx = counts[0]
    full_x = tx * nx
    own = ty // nx
    rows = own + 2 * DEEP
    gx, gy, gz = [lax.axis_index(a) for a in AXES]

    ny = counts[1]
    slabs = nx * ny
    place = gx * ny + gy
    source_y = place // nx
    my_part = place % nx
    inner = source_y == gy

    def slab_device(s, z):
        return (s // ny, s % ny, z)

    def target(t):
        return slab_device(gy * nx + t, gz)

    def apart(t):
        return gy * nx + t != place

    def distant(i):
        return (gx != i) | (gy != source_y)

    hops = [(dy, dz) for dy in (-1, 0, 1) for dz in (-1, 0, 1) if dy or dz]

    def exists(dy, dz):
        s, z = place + dy, gz + dz
        return (s >= 0) & (s < slabs) & (z >= 0) & (z < counts[2])

    def device(dy, dz):
        s = jnp.clip(place + dy, 0, slabs - 1)
        z = jnp.clip(gz + dz, 0, counts[2] - 1)
        return slab_device(s, z)

    def other(d):
        return lax.rem(gx + d, nx)

    fetches = [
        pltpu.make_async_copy(src, dst, fetch_sem.at[i])
        for i, (src, dst) in enumerate(
            (
                (courant_ref, mine.at[2]),
                (top_ref, tops),
                (thick_ref, thicks),
                (before_ref, mine.at[0]),
                (now_ref, mine.at[1]),
            )
        )
    ]
    for c in fetches:
        c.start()

    field[...] = jnp.zeros_like(field)
    land_y[...] = jnp.zeros_like(land_y)
    land_z[...] = jnp.zeros_like(land_z)

    barrier = pltpu.get_barrier_semaphore()
    on_top = gz == 0
    own_receivers = [
        pltpu.make_async_copy(trace_ref, traces.at[0], gather_send.at[0, 0]),
        pltpu.make_async_copy(tag_ref, tags.at[0], gather_send.at[0, 1]),
    ]
    for d in range(1, nx):
        pl.semaphore_signal(barrier, inc=1, device_id=(other(d), gy, gz), device_id_type=MESH)
    for t in range(nx):

        @pl.when(apart(t))
        def _():
            pl.semaphore_signal(barrier, inc=1, device_id=target(t), device_id_type=MESH)

        @pl.when(distant(t))
        def _():
            pl.semaphore_signal(barrier, inc=1, device_id=(t, source_y, gz), device_id_type=MESH)

    greeted = nx - 1 + 2 * (nx - inner.astype(jnp.int32))
    for hop in hops:
        greeted = greeted + exists(*hop).astype(jnp.int32)

        @pl.when(exists(*hop))
        def _():
            pl.semaphore_signal(barrier, inc=1, device_id=device(*hop), device_id_type=MESH)

    for c in own_receivers:
        c.start()
    for c in fetches:
        c.wait()
    half_y = ty // 2
    pick = lax.broadcasted_iota(jnp.int32, (ty, half_y), 0) // 2 == lax.broadcasted_iota(
        jnp.int32, (ty, half_y), 1
    )
    depth = (gz * tz + lax.broadcasted_iota(jnp.int32, (ty, tz), 1)).astype(jnp.float32)
    for xb in range(tx // 2):
        top_row = tops[xb : xb + 1, :].astype(jnp.float32)
        thick_row = thicks[xb : xb + 1, :].astype(jnp.float32)
        top = jnp.sum(jnp.where(pick, top_row, 0.0), axis=1, keepdims=True)
        end = top + jnp.sum(jnp.where(pick, thick_row, 0.0), axis=1, keepdims=True)
        solid = (depth >= top) & (depth < end)
        for x in (2 * xb, 2 * xb + 1):
            mine[2, x] = jnp.where(solid, 0.0, mine[2, x])

    pl.semaphore_wait(barrier, greeted)

    def swap(t, i):
        return pltpu.make_async_remote_copy(
            src_ref=mine.at[:, :, pl.ds(t * own, own), :],
            dst_ref=field.at[:, pl.ds(gx * tx, tx), pl.ds(DEEP, own), pl.ds(0, tz)],
            send_sem=swap_send.at[t],
            recv_sem=swap_recv.at[i],
            device_id=target(t),
            device_id_type=MESH,
        )

    def gather(d):
        pair = []
        for k, (src, dst) in enumerate(((trace_ref, traces), (tag_ref, tags))):
            pair.append(
                pltpu.make_async_remote_copy(
                    src_ref=src,
                    dst_ref=dst.at[d],
                    send_sem=gather_send.at[d, k],
                    recv_sem=gather_recv.at[d, k],
                    device_id=(other(d), gy, gz),
                    device_id_type=MESH,
                )
            )
        return pair

    for t in range(nx):

        @pl.when(apart(t))
        def _():
            swap(t, gx).start()

    @pl.when(on_top)
    def _():
        for d in range(1, nx):
            for c in gather(d):
                c.start()

    first = pl.multiple_of(my_part * own, 8)

    @pl.when(inner)
    def _():
        for x in range(tx):
            field[:, gx * tx + x, DEEP : DEEP + own, 0:tz] = mine[:, x, pl.ds(first, own), :]

    lane = lax.broadcasted_iota(jnp.int32, (own, tz), 1)
    tall_lane = lax.broadcasted_iota(jnp.int32, (rows, tz), 1)

    def halo(hop, slot, fields):
        dy, dz = hop
        k = hops.index(hop)
        if dz == 0:
            src = field.at[
                pl.ds(0, fields), :, pl.ds(DEEP if dy < 0 else own, DEEP), pl.ds(0, tz)
            ]
            dst = land_y.at[slot, 1 if dy < 0 else 0, pl.ds(0, fields)]
        else:
            from_row, to_row, size = {
                -1: (0, DEEP + own, DEEP),
                0: (0, DEEP, own),
                1: (own - DEEP, 0, DEEP),
            }[dy]
            src = send_z.at[1 if dz > 0 else 0, pl.ds(0, fields), pl.ds(from_row, size)]
            dst = land_z.at[slot, 1 if dz < 0 else 0, pl.ds(0, fields), pl.ds(to_row, size)]
        return pltpu.make_async_remote_copy(
            src_ref=src,
            dst_ref=dst,
            send_sem=halo_send.at[k, slot],
            recv_sem=halo_recv.at[k, slot],
            device_id=device(dy, dz),
            device_id_type=MESH,
        )

    def send_halos(slot, fields):
        for hop in hops:
            if hop[1] == 0:

                @pl.when(exists(*hop))
                def _():
                    halo(hop, slot, fields).start()

        for f in range(fields):
            low = jnp.zeros((own, tz), jnp.float32)
            high = jnp.zeros((own, tz), jnp.float32)
            for x in range(full_x):
                part = field[f, x, DEEP : DEEP + own, 0:tz]
                at = x * DEEP
                here = (lane >= at) & (lane < at + DEEP)
                low = jnp.where(here, pltpu.roll(part, at, 1) if at else part, low)
                turn = (at + DEEP) % tz
                high = jnp.where(here, pltpu.roll(part, turn, 1) if turn else part, high)
            send_z[0, f] = low
            send_z[1, f] = high
        for hop in hops:
            if hop[1] != 0:

                @pl.when(exists(*hop))
                def _():
                    halo(hop, slot, fields).start()

    def take_halos(slot, fields):
        for hop in hops:

            @pl.when(exists(-hop[0], -hop[1]))
            def _():
                halo(hop, slot, fields).wait_recv()

        for hop in hops:

            @pl.when(exists(*hop))
            def _():
                halo(hop, slot, fields).wait_send()

        for f in range(fields):
            from_low = land_z[slot, 0, f]
            from_high = land_z[slot, 1, f]
            for x in range(full_x):
                field[f, x, 0:DEEP, 0:tz] = land_y[slot, 0, f, x]
                field[f, x, DEEP + own : rows, 0:tz] = land_y[slot, 1, f, x]
                right = pltpu.roll(from_high, (tz - x * DEEP) % tz, 1) if x else from_high
                turn = (2 * tz - DEEP - x * DEEP) % tz
                left = pltpu.roll(from_low, turn, 1) if turn else from_low
                field[f, x, :, tz : 2 * tz] = jnp.where(
                    tall_lane < DEEP, right, jnp.where(tall_lane >= tz - DEEP, left, 0.0)
                )

    for i in range(nx):

        @pl.when(distant(i))
        def _():
            swap(0, i).wait_recv()

    send_halos(0, 3)

    cells = full_x * rows
    row = lax.broadcasted_iota(jnp.int32, (cells, tag_ref.shape[1]), 0)

    def receivers(tag, trace):
        cell = tag[0:1, :]
        kind = tag[1:2, :]
        weight = jnp.zeros(kind.shape, jnp.float32)
        for c in range(table_ref.shape[0]):
            weight = jnp.where(kind == c, table_ref[c], weight)
        y = cell % grid_y - place * own + DEEP
        seg = jnp.where((y >= 0) & (y < rows), cell // grid_y * rows + y, -1)
        hit = jnp.where(row == seg, 1.0, 0.0).astype(jnp.bfloat16)
        left = weight * trace.astype(jnp.float32)
        total = None
        for _ in range(3):
            piece = left.astype(jnp.bfloat16)
            left = left - piece.astype(jnp.float32)
            term = lax.dot_general(
                hit, piece, (((1,), (1,)), ((), ())), preferred_element_type=jnp.float32
            )
            total = term if total is None else total + term
        return total

    sources[...] = jnp.zeros_like(sources)
    for c in own_receivers:
        c.wait()

    @pl.when(on_top)
    def _():
        total = receivers(tags[0], traces[0])
        for d in range(1, nx):
            for c in gather(d):
                c.wait()
            total = total + receivers(tags[d], traces[d])
        for x in range(full_x):
            sources[x, :, 0:steps] = total[x * rows : (x + 1) * rows]

    for t in range(nx):

        @pl.when(apart(t))
        def _():
            swap(t, gx).wait_send()

    wide = 2 * tz

    def step(n, current):
        new = 1 - current
        turn = lax.rem(n + 1 - steps + tz, tz)
        for x in range(full_x):
            c = field[current, x]
            around = pltpu.roll(c, 1, 0) + pltpu.roll(c, rows - 1, 0)
            around = around + (pltpu.roll(c, 1, 1) + pltpu.roll(c, wide - 1, 1))
            if x > 0:
                around = around + field[current, x - 1]
            if x < full_x - 1:
                around = around + field[current, x + 1]
            speed = field[2, x]
            source = jnp.where(tall_lane == 0, pltpu.roll(sources[x], turn, 1), 0.0)
            source = jnp.concatenate([source, jnp.zeros_like(source)], axis=1)
            updated = 2.0 * c - field[new, x] + speed * (around - 6.0 * c) + source
            field[new, x] = jnp.where(speed > 0.0, updated, 0.0)

    def advance(r):
        def double_step(k, carry):
            step(r * DEEP + 2 * k, 1)
            step(r * DEEP + 2 * k + 1, 0)
            return carry

        lax.fori_loop(0, DEEP // 2, double_step, 0)

    take_halos(0, 3)
    advance(0)

    def round_of(r, carry):
        slot = r % 2
        send_halos(slot, 2)
        take_halos(slot, 2)
        advance(r)
        return carry

    lax.fori_loop(1, steps // DEEP, round_of, 0)

    def back(i, part):
        return pltpu.make_async_remote_copy(
            src_ref=field.at[1, pl.ds(i * tx, tx), pl.ds(DEEP, own), pl.ds(0, tz)],
            dst_ref=result.at[:, pl.ds(first, own), :],
            send_sem=back_send.at[i],
            recv_sem=back_recv.at[part],
            device_id=(i, source_y, gz),
            device_id_type=MESH,
        )

    for i in range(nx):

        @pl.when(distant(i))
        def _():
            back(i, my_part).start()

    @pl.when(inner)
    def _():
        for x in range(tx):
            result[x, pl.ds(first, own), :] = field[1, gx * tx + x, DEEP : DEEP + own, 0:tz]

    for t in range(nx):

        @pl.when(apart(t))
        def _():
            back(0, t).wait_recv()

    for i in range(nx):

        @pl.when(distant(i))
        def _():
            back(i, my_part).wait_send()

    out_ref[...] = result[...]


def slab_scratch(counts, tx, ty, tz, count, steps):
    nx = counts[0]
    own = ty // nx
    rows = own + 2 * DEEP
    full_x = tx * nx
    sem = pltpu.SemaphoreType.DMA
    return [
        pltpu.VMEM((3, full_x, rows, 2 * tz), jnp.float32),
        pltpu.VMEM((3, tx, ty, tz), jnp.float32),
        pltpu.VMEM((2, 2, 3, full_x, DEEP, tz), jnp.float32),
        pltpu.VMEM((2, 2, 3, rows, tz), jnp.float32),
        pltpu.VMEM((2, 3, own, tz), jnp.float32),
        pltpu.VMEM((full_x, rows, tz), jnp.float32),
        pltpu.VMEM((nx, steps, count), jnp.bfloat16),
        pltpu.VMEM((nx, 2, count), jnp.int32),
        pltpu.VMEM((tx, ty, tz), jnp.float32),
        sem((8, 2)),
        sem((8, 2)),
        sem((nx,)),
        sem((nx,)),
        sem((nx, 2)),
        sem((nx, 2)),
        sem((nx,)),
        sem((nx,)),
        pltpu.VMEM((tx // 2, ty // 2), jnp.int32),
        pltpu.VMEM((tx // 2, ty // 2), jnp.int32),
        sem((5,)),
    ]


def slabs_fit(counts, tx, ty, tz, steps):
    own = ty // counts[0]
    return (
        own * counts[0] == ty
        and own % DEEP == 0
        and tx * counts[0] * DEEP == tz
        and steps % DEEP == 0
        and steps <= tz
    )


def face_scratch(counts, tx, ty, tz, count, steps):
    others = max(counts[0] - 1, 1)
    return [
        pltpu.VMEM((2, tx, ty, tz), jnp.float32),
        pltpu.VMEM((2, 2, ty, tz), jnp.float32),
        pltpu.VMEM((2, 2, tx, tz), jnp.float32),
        pltpu.VMEM((2, 2, 8, tz), jnp.float32),
        pltpu.VMEM((2, 2, tx, tz), jnp.float32),
        pltpu.VMEM((2, 2, 8, tz), jnp.float32),
        pltpu.VMEM((tx, ty, tz), jnp.float32),
        pltpu.VMEM((tx, ty, tz), jnp.float32),
        pltpu.VMEM((others, steps, count), jnp.bfloat16),
        pltpu.VMEM((others, 2, count), jnp.int32),
        pltpu.SemaphoreType.DMA((6, 2)),
        pltpu.SemaphoreType.DMA((6, 2)),
        pltpu.SemaphoreType.DMA((others, 2)),
        pltpu.SemaphoreType.DMA((others, 2)),
    ]


def local(counts, traces, receiver_cell, weight_class, weight_table, top, thick, courant, now, before):
    tx, ty, tz = courant.shape
    count, steps = traces.shape
    tag = jnp.stack([receiver_cell, weight_class])
    vmem = pl.BlockSpec(memory_space=pltpu.VMEM)
    smem = pl.BlockSpec(memory_space=pltpu.SMEM)
    if slabs_fit(counts, tx, ty, tz, steps):
        body, number, place = slab_kernel, 1, pl.BlockSpec(memory_space=pl.ANY)
        scratch = slab_scratch(counts, tx, ty, tz, count, steps)
    else:
        body, number, place = kernel, 0, vmem
        scratch = face_scratch(counts, tx, ty, tz, count, steps)
    return pl.pallas_call(
        functools.partial(body, counts, ty * counts[1], steps),
        out_shape=jax.ShapeDtypeStruct((tx, ty, tz), jnp.float32),
        in_specs=[place, place, smem, place, place, place, place, place],
        out_specs=vmem,
        scratch_shapes=scratch,
        compiler_params=pltpu.CompilerParams(
            collective_id=number, has_side_effects=True, vmem_limit_bytes=56 * 1024 * 1024
        ),
    )(traces.T, tag, weight_table, top, thick, courant, now, before)


def solution(mesh):
    counts = tuple(mesh.shape[a] for a in AXES)
    tile = P("gx", "gy", "gz")
    columns = P("gx", "gy")
    placed = (P("gx", None), P("gx"), P("gx"), P(), columns, columns, tile, tile, tile)
    return jax.shard_map(
        functools.partial(local, counts), mesh=mesh, in_specs=placed, out_specs=tile, check_vma=False
    )
```

```python
import functools

import jax
import jax.numpy as jnp
from jax import lax
from jax.experimental import pallas as pl
from jax.experimental.pallas import tpu as pltpu
from jax.sharding import PartitionSpec as P

MESH = pl.DeviceIdType.MESH
AXES = ("gx", "gy", "gz")


def kernel(
    counts,
    grid_y,
    steps,
    trace_ref,
    tag_ref,
    table_ref,
    top_ref,
    thick_ref,
    courant_ref,
    now_ref,
    before_ref,
    out_ref,
    field,
    ghost_x,
    ghost_y,
    ghost_z,
    send_y,
    send_z,
    living,
    sources,
    traces,
    tags,
    send_sem,
    recv_sem,
    gather_send,
    gather_recv,
):
    tx, ty, tz = courant_ref.shape
    rows = ty // 8
    me = [lax.axis_index(a) for a in AXES]
    has_lo = [me[a] > 0 for a in range(3)]
    has_hi = [me[a] < counts[a] - 1 for a in range(3)]
    lo_id = [{AXES[a]: jnp.maximum(me[a] - 1, 0)} for a in range(3)]
    hi_id = [{AXES[a]: jnp.minimum(me[a] + 1, counts[a] - 1)} for a in range(3)]

    def copy(direction, slot):
        axis, upper = direction // 2, direction % 2
        if axis == 0:
            src = field.at[slot, tx - 1 if upper else 0]
            dst = ghost_x.at[slot, direction % 2]
        elif axis == 1:
            src = send_y.at[slot, upper]
            dst = ghost_y.at[slot, upper]
        else:
            src = send_z.at[slot, upper]
            dst = ghost_z.at[slot, upper]
        return pltpu.make_async_remote_copy(
            src_ref=src,
            dst_ref=dst,
            send_sem=send_sem.at[direction, slot],
            recv_sem=recv_sem.at[direction, slot],
            device_id=(hi_id if upper else lo_id)[axis],
            device_id_type=MESH,
        )

    def target(direction):
        return (has_hi if direction % 2 else has_lo)[direction // 2]

    def origin(direction):
        return (has_lo if direction % 2 else has_hi)[direction // 2]

    def start(direction, slot, also=None):
        cond = target(direction) if also is None else target(direction) & also

        @pl.when(cond)
        def _():
            copy(direction, slot).start()

    def wait_recv(direction, slot):
        @pl.when(origin(direction))
        def _():
            copy(direction, slot).wait_recv()

    def wait_send(direction, slot):
        @pl.when(target(direction))
        def _():
            copy(direction, slot).wait_send()

    ghost_x[...] = jnp.zeros_like(ghost_x)
    ghost_y[...] = jnp.zeros_like(ghost_y)
    ghost_z[...] = jnp.zeros_like(ghost_z)
    field[0] = now_ref[...]
    field[1] = before_ref[...]

    barrier = pltpu.get_barrier_semaphore()
    for d in range(1, counts[0]):
        pl.semaphore_signal(
            barrier,
            inc=1,
            device_id={"gx": lax.rem(me[0] + d, counts[0])},
            device_id_type=MESH,
        )
    for axis in (1, 2):

        @pl.when(has_lo[axis])
        def _():
            pl.semaphore_signal(barrier, inc=1, device_id=lo_id[axis], device_id_type=MESH)

        @pl.when(has_hi[axis])
        def _():
            pl.semaphore_signal(barrier, inc=1, device_id=hi_id[axis], device_id_type=MESH)

    greeted = counts[0] - 1
    for axis in (1, 2):
        greeted = greeted + has_lo[axis].astype(jnp.int32) + has_hi[axis].astype(jnp.int32)

    lane = lax.broadcasted_iota(jnp.int32, (8, tz), 1)

    def pack_z(slot):
        low = jnp.zeros((8, tz), jnp.float32)
        high = jnp.zeros((8, tz), jnp.float32)
        for x in range(tx):
            for b in range(rows):
                j = x * rows + b
                part = field[slot, x, b * 8 : b * 8 + 8, :]
                low = jnp.where(lane == j, pltpu.roll(part, j, 1) if j else part, low)
                high = jnp.where(lane == j, pltpu.roll(part, j + 1, 1), high)
        send_z[slot, 0] = low
        send_z[slot, 1] = high

    def pack_y(slot):
        for x in range(tx):
            send_y[slot, 0, x : x + 1, :] = field[slot, x, 0:1, :]
            send_y[slot, 1, x : x + 1, :] = field[slot, x, ty - 1 : ty, :]

    pack_y(0)
    pack_z(0)
    pl.semaphore_wait(barrier, greeted)
    for direction in range(6):
        start(direction, 0)

    def gather(d):
        there = {"gx": lax.rem(me[0] + d, counts[0])}
        pair = []
        for k, (src, dst) in enumerate(((trace_ref, traces), (tag_ref, tags))):
            pair.append(
                pltpu.make_async_remote_copy(
                    src_ref=src,
                    dst_ref=dst.at[d - 1],
                    send_sem=gather_send.at[d - 1, k],
                    recv_sem=gather_recv.at[d - 1, k],
                    device_id=there,
                    device_id_type=MESH,
                )
            )
        return pair

    for d in range(1, counts[0]):
        for c in gather(d):
            c.start()

    half_y = ty // 2
    pick = lax.broadcasted_iota(jnp.int32, (ty, half_y), 0) // 2 == lax.broadcasted_iota(
        jnp.int32, (ty, half_y), 1
    )
    depth = (me[2] * tz + lax.broadcasted_iota(jnp.int32, (ty, tz), 1)).astype(jnp.float32)
    for xb in range(tx // 2):
        top_row = top_ref[xb : xb + 1, :].astype(jnp.float32)
        thick_row = thick_ref[xb : xb + 1, :].astype(jnp.float32)
        top = jnp.sum(jnp.where(pick, top_row, 0.0), axis=1, keepdims=True)
        end = top + jnp.sum(jnp.where(pick, thick_row, 0.0), axis=1, keepdims=True)
        alive = jnp.where((depth >= top) & (depth < end), 0.0, 1.0)
        living[2 * xb] = alive
        living[2 * xb + 1] = alive

    cells = tx * ty
    row = lax.broadcasted_iota(jnp.int32, (cells, tag_ref.shape[1]), 0)
    surface = (me[2] == 0).astype(jnp.float32)

    def receivers(tag, trace):
        cell = tag[0:1, :]
        kind = tag[1:2, :]
        weight = jnp.zeros(kind.shape, jnp.float32)
        for c in range(table_ref.shape[0]):
            weight = jnp.where(kind == c, table_ref[c], weight)
        x = cell // grid_y - me[0] * tx
        y = cell % grid_y - me[1] * ty
        inside = (x >= 0) & (x < tx) & (y >= 0) & (y < ty)
        seg = jnp.where(inside, x * ty + y, -1)
        hit = row == seg
        total = None
        for _ in range(3):
            piece = weight.astype(jnp.bfloat16).astype(jnp.float32)
            weight = weight - piece
            spread = jnp.where(hit, piece, 0.0).astype(jnp.bfloat16)
            term = lax.dot_general(
                spread, trace, (((1,), (1,)), ((), ())), preferred_element_type=jnp.float32
            )
            total = term if total is None else total + term
        return total

    total = receivers(tag_ref[...], trace_ref[...])
    for d in range(1, counts[0]):
        for c in gather(d):
            c.wait()
        total = total + receivers(tags[d - 1], traces[d - 1])
    total = total * surface
    sources[...] = jnp.zeros_like(sources)
    for x in range(tx):
        sources[x, :, 0:steps] = total[x * ty : (x + 1) * ty]

    wide_lane = lax.broadcasted_iota(jnp.int32, (ty, tz), 1)
    wide_row = lax.broadcasted_iota(jnp.int32, (ty, tz), 0)

    def step(n, slot):
        new = 1 - slot
        more = n < steps - 1
        for direction in (2, 3, 4, 5):
            wait_recv(direction, slot)
        z_low = ghost_z[slot, 1]
        z_high = ghost_z[slot, 0]

        def plane(x, below, above):
            c = field[slot, x]
            y_low = jnp.where(wide_row == 0, ghost_y[slot, 1, x : x + 1, :], pltpu.roll(c, 1, 0))
            y_high = jnp.where(
                wide_row == ty - 1, ghost_y[slot, 0, x : x + 1, :], pltpu.roll(c, ty - 1, 0)
            )
            low_parts, high_parts = [], []
            for b in range(rows):
                j = x * rows + b
                low_parts.append(pltpu.roll(z_low, (tz - j) % tz, 1) if j else z_low)
                high_parts.append(pltpu.roll(z_high, tz - 1 - j, 1))
            left = jnp.where(
                wide_lane == 0, jnp.concatenate(low_parts, axis=0), pltpu.roll(c, 1, 1)
            )
            right = jnp.where(
                wide_lane == tz - 1, jnp.concatenate(high_parts, axis=0), pltpu.roll(c, tz - 1, 1)
            )
            laplace = above + below + y_high + y_low + right + left - 6.0 * c
            source = pltpu.roll(sources[x], lax.rem(n + 1 - steps + tz, tz), 1)
            source = jnp.where(wide_lane == 0, source, 0.0)
            updated = 2.0 * c - field[new, x] + courant_ref[x] * laplace + source
            field[new, x] = living[x] * updated

        for x in range(1, tx - 1):
            plane(x, field[slot, x - 1], field[slot, x + 1])
        wait_recv(1, slot)
        plane(0, ghost_x[slot, 1], field[slot, 1])
        start(0, new, more)
        wait_recv(0, slot)
        plane(tx - 1, field[slot, tx - 2], ghost_x[slot, 0])
        start(1, new, more)
        pack_y(new)
        start(2, new, more)
        start(3, new, more)
        pack_z(new)
        start(4, new, more)
        start(5, new, more)
        for direction in range(6):
            wait_send(direction, slot)

    def double_step(k, carry):
        step(2 * k, 0)
        step(2 * k + 1, 1)
        return carry

    lax.fori_loop(0, steps // 2, double_step, 0)
    out_ref[...] = field[0]

DEEP = 8


def slab_kernel(
    counts,
    grid_y,
    steps,
    trace_ref,
    cell_ref,
    class_ref,
    table_ref,
    top_ref,
    thick_ref,
    courant_ref,
    now_ref,
    before_ref,
    out_ref,
    field,
    mine,
    land_y,
    land_z,
    send_z,
    sources,
    traces,
    cell_rows,
    class_rows,
    result,
    halo_send,
    halo_recv,
    swap_send,
    swap_recv,
    gather_send,
    gather_recv,
    back_send,
    back_recv,
    tops,
    thicks,
    fetch_sem,
):
    tx, ty, tz = courant_ref.shape
    nx = counts[0]
    full_x = tx * nx
    own = ty // nx
    rows = own + 2 * DEEP
    gx, gy, gz = [lax.axis_index(a) for a in AXES]

    ny = counts[1]
    slabs = nx * ny
    place = gx * ny + gy
    source_y = place // nx
    my_part = place % nx
    inner = source_y == gy

    def slab_device(s, z):
        return (s // ny, s % ny, z)

    def target(t):
        return slab_device(gy * nx + t, gz)

    def apart(t):
        return gy * nx + t != place

    def distant(i):
        return (gx != i) | (gy != source_y)

    hops = [(dy, dz) for dy in (-1, 0, 1) for dz in (-1, 0, 1) if dy or dz]

    def exists(dy, dz):
        s, z = place + dy, gz + dz
        return (s >= 0) & (s < slabs) & (z >= 0) & (z < counts[2])

    def device(dy, dz):
        s = jnp.clip(place + dy, 0, slabs - 1)
        z = jnp.clip(gz + dz, 0, counts[2] - 1)
        return slab_device(s, z)

    def other(d):
        return lax.rem(gx + d, nx)

    fetches = [
        pltpu.make_async_copy(src, dst, fetch_sem.at[i])
        for i, (src, dst) in enumerate(
            (
                (before_ref, mine.at[0]),
                (now_ref, mine.at[1]),
                (top_ref, tops),
                (thick_ref, thicks),
                (courant_ref, mine.at[2]),
            )
        )
    ]
    for c in fetches:
        c.start()

    field[...] = jnp.zeros_like(field)
    land_y[...] = jnp.zeros_like(land_y)
    land_z[...] = jnp.zeros_like(land_z)

    barrier = pltpu.get_barrier_semaphore()
    on_top = gz == 0
    own_receivers = [
        pltpu.make_async_copy(trace_ref, traces.at[0], gather_send.at[0, 0]),
        pltpu.make_async_copy(cell_ref, cell_rows.at[0], gather_send.at[0, 1]),
        pltpu.make_async_copy(class_ref, class_rows.at[0], gather_send.at[0, 2]),
    ]
    for d in range(1, nx):
        pl.semaphore_signal(barrier, inc=1, device_id=(other(d), gy, gz), device_id_type=MESH)
    for t in range(nx):

        @pl.when(apart(t))
        def _():
            pl.semaphore_signal(barrier, inc=1, device_id=target(t), device_id_type=MESH)

        @pl.when(distant(t))
        def _():
            pl.semaphore_signal(barrier, inc=1, device_id=(t, source_y, gz), device_id_type=MESH)

    greeted = nx - 1 + 2 * (nx - inner.astype(jnp.int32))
    for hop in hops:
        greeted = greeted + exists(*hop).astype(jnp.int32)

        @pl.when(exists(*hop))
        def _():
            pl.semaphore_signal(barrier, inc=1, device_id=device(*hop), device_id_type=MESH)

    for c in own_receivers:
        c.start()
    for c in fetches[:2]:
        c.wait()
    pl.semaphore_wait(barrier, greeted)

    def swap(t, i, part):
        some = pl.ds(2 * part, 2 - part)
        return pltpu.make_async_remote_copy(
            src_ref=mine.at[some, :, pl.ds(t * own, own), :],
            dst_ref=field.at[some, pl.ds(gx * tx, tx), pl.ds(DEEP, own), pl.ds(0, tz)],
            send_sem=swap_send.at[t, part],
            recv_sem=swap_recv.at[i, part],
            device_id=target(t),
            device_id_type=MESH,
        )

    def gather(d):
        pair = []
        for k, (src, dst) in enumerate(((trace_ref, traces), (cell_ref, cell_rows), (class_ref, class_rows))):
            pair.append(
                pltpu.make_async_remote_copy(
                    src_ref=src,
                    dst_ref=dst.at[d],
                    send_sem=gather_send.at[d, k],
                    recv_sem=gather_recv.at[d, k],
                    device_id=(other(d), gy, gz),
                    device_id_type=MESH,
                )
            )
        return pair

    for t in range(nx):

        @pl.when(apart(t))
        def _():
            swap(t, gx, 0).start()

    @pl.when(on_top)
    def _():
        for d in range(1, nx):
            for c in gather(d):
                c.start()

    for c in fetches[2:]:
        c.wait()
    half_y = ty // 2
    pick = lax.broadcasted_iota(jnp.int32, (ty, half_y), 0) // 2 == lax.broadcasted_iota(
        jnp.int32, (ty, half_y), 1
    )
    depth = (gz * tz + lax.broadcasted_iota(jnp.int32, (ty, tz), 1)).astype(jnp.float32)
    for xb in range(tx // 2):
        top_row = tops[xb : xb + 1, :].astype(jnp.float32)
        thick_row = thicks[xb : xb + 1, :].astype(jnp.float32)
        top = jnp.sum(jnp.where(pick, top_row, 0.0), axis=1, keepdims=True)
        end = top + jnp.sum(jnp.where(pick, thick_row, 0.0), axis=1, keepdims=True)
        solid = (depth >= top) & (depth < end)
        for x in (2 * xb, 2 * xb + 1):
            mine[2, x] = jnp.where(solid, 0.0, mine[2, x])

    for t in range(nx):

        @pl.when(apart(t))
        def _():
            swap(t, gx, 1).start()

    first = pl.multiple_of(my_part * own, 8)

    @pl.when(inner)
    def _():
        for x in range(tx):
            field[:, gx * tx + x, DEEP : DEEP + own, 0:tz] = mine[:, x, pl.ds(first, own), :]

    lane = lax.broadcasted_iota(jnp.int32, (own, tz), 1)
    tall_lane = lax.broadcasted_iota(jnp.int32, (rows, tz), 1)

    def halo(hop, slot, low_field, fields, sem):
        dy, dz = hop
        k = hops.index(hop)
        some = pl.ds(low_field, fields)
        if dz == 0:
            src = field.at[
                pl.ds(low_field, fields), :, pl.ds(DEEP if dy < 0 else own, DEEP), pl.ds(0, tz)
            ]
            dst = land_y.at[slot, 1 if dy < 0 else 0, pl.ds(low_field, fields)]
        else:
            from_row, to_row, size = {
                -1: (0, DEEP + own, DEEP),
                0: (0, DEEP, own),
                1: (own - DEEP, 0, DEEP),
            }[dy]
            src = send_z.at[1 if dz > 0 else 0, some, pl.ds(from_row, size)]
            dst = land_z.at[slot, 1 if dz < 0 else 0, some, pl.ds(to_row, size)]
        return pltpu.make_async_remote_copy(
            src_ref=src,
            dst_ref=dst,
            send_sem=halo_send.at[k, sem],
            recv_sem=halo_recv.at[k, sem],
            device_id=device(dy, dz),
            device_id_type=MESH,
        )

    def send_halos(slot, low_field, fields, sem):
        for hop in hops:
            if hop[1] == 0:

                @pl.when(exists(*hop))
                def _():
                    halo(hop, slot, low_field, fields, sem).start()

        for f in range(low_field, low_field + fields):
            low = jnp.zeros((own, tz), jnp.float32)
            high = jnp.zeros((own, tz), jnp.float32)
            for x in range(full_x):
                part = field[f, x, DEEP : DEEP + own, 0:tz]
                at = x * DEEP
                here = (lane >= at) & (lane < at + DEEP)
                low = jnp.where(here, pltpu.roll(part, at, 1) if at else part, low)
                turn = (at + DEEP) % tz
                high = jnp.where(here, pltpu.roll(part, turn, 1) if turn else part, high)
            send_z[0, f] = low
            send_z[1, f] = high
        for hop in hops:
            if hop[1] != 0:

                @pl.when(exists(*hop))
                def _():
                    halo(hop, slot, low_field, fields, sem).start()

    def take_halos(slot, low_field, fields, sem):
        for hop in hops:

            @pl.when(exists(-hop[0], -hop[1]))
            def _():
                halo(hop, slot, low_field, fields, sem).wait_recv()

        for hop in hops:

            @pl.when(exists(*hop))
            def _():
                halo(hop, slot, low_field, fields, sem).wait_send()

        for f in range(low_field, low_field + fields):
            from_low = land_z[slot, 0, f]
            from_high = land_z[slot, 1, f]
            for x in range(full_x):
                field[f, x, 0:DEEP, 0:tz] = land_y[slot, 0, f, x]
                field[f, x, DEEP + own : rows, 0:tz] = land_y[slot, 1, f, x]
                right = pltpu.roll(from_high, (tz - x * DEEP) % tz, 1) if x else from_high
                turn = (2 * tz - DEEP - x * DEEP) % tz
                left = pltpu.roll(from_low, turn, 1) if turn else from_low
                field[f, x, :, tz : 2 * tz] = jnp.where(
                    tall_lane < DEEP, right, jnp.where(tall_lane >= tz - DEEP, left, 0.0)
                )

    for i in range(nx):

        @pl.when(distant(i))
        def _():
            swap(0, i, 0).wait_recv()

    send_halos(0, 0, 2, 0)
    for i in range(nx):

        @pl.when(distant(i))
        def _():
            swap(0, i, 1).wait_recv()

    send_halos(0, 2, 1, 2)

    cells = full_x * rows
    row = lax.broadcasted_iota(jnp.int32, (cells, trace_ref.shape[1]), 0)

    def receivers(cell, kind, trace):
        weight = jnp.zeros(kind.shape, jnp.float32)
        for c in range(table_ref.shape[0]):
            weight = jnp.where(kind == c, table_ref[c], weight)
        y = cell % grid_y - place * own + DEEP
        seg = jnp.where((y >= 0) & (y < rows), cell // grid_y * rows + y, -1)
        hit = jnp.where(row == seg, 1.0, 0.0).astype(jnp.bfloat16)
        left = weight * trace.astype(jnp.float32)
        total = None
        for _ in range(3):
            piece = left.astype(jnp.bfloat16)
            left = left - piece.astype(jnp.float32)
            term = lax.dot_general(
                hit, piece, (((1,), (1,)), ((), ())), preferred_element_type=jnp.float32
            )
            total = term if total is None else total + term
        return total

    sources[...] = jnp.zeros_like(sources)
    for c in own_receivers:
        c.wait()

    @pl.when(on_top)
    def _():
        total = receivers(cell_rows[0], class_rows[0], traces[0])
        for d in range(1, nx):
            for c in gather(d):
                c.wait()
            total = total + receivers(cell_rows[d], class_rows[d], traces[d])
        for x in range(full_x):
            sources[x, :, 0:steps] = total[x * rows : (x + 1) * rows]

    for t in range(nx):

        @pl.when(apart(t))
        def _():
            swap(t, gx, 0).wait_send()
            swap(t, gx, 1).wait_send()

    wide = 2 * tz

    def step(n, current):
        new = 1 - current
        turn = lax.rem(n + 1 - steps + tz, tz)
        for x in range(full_x):
            c = field[current, x]
            around = pltpu.roll(c, 1, 0) + pltpu.roll(c, rows - 1, 0)
            around = around + (pltpu.roll(c, 1, 1) + pltpu.roll(c, wide - 1, 1))
            if x > 0:
                around = around + field[current, x - 1]
            if x < full_x - 1:
                around = around + field[current, x + 1]
            speed = field[2, x]
            source = jnp.where(tall_lane == 0, pltpu.roll(sources[x], turn, 1), 0.0)
            source = jnp.concatenate([source, jnp.zeros_like(source)], axis=1)
            updated = 2.0 * c - field[new, x] + speed * (around - 6.0 * c) + source
            field[new, x] = jnp.where(speed > 0.0, updated, 0.0)

    def advance(r):
        def double_step(k, carry):
            step(r * DEEP + 2 * k, 1)
            step(r * DEEP + 2 * k + 1, 0)
            return carry

        lax.fori_loop(0, DEEP // 2, double_step, 0)

    take_halos(0, 0, 2, 0)
    take_halos(0, 2, 1, 2)
    advance(0)

    def round_of(r, carry):
        slot = r % 2
        send_halos(slot, 0, 2, slot)
        take_halos(slot, 0, 2, slot)
        advance(r)
        return carry

    lax.fori_loop(1, steps // DEEP, round_of, 0)

    def back(i, part):
        return pltpu.make_async_remote_copy(
            src_ref=field.at[1, pl.ds(i * tx, tx), pl.ds(DEEP, own), pl.ds(0, tz)],
            dst_ref=result.at[:, pl.ds(first, own), :],
            send_sem=back_send.at[i],
            recv_sem=back_recv.at[part],
            device_id=(i, source_y, gz),
            device_id_type=MESH,
        )

    for i in range(nx):

        @pl.when(distant(i))
        def _():
            back(i, my_part).start()

    @pl.when(inner)
    def _():
        for x in range(tx):
            result[x, pl.ds(first, own), :] = field[1, gx * tx + x, DEEP : DEEP + own, 0:tz]

    for t in range(nx):

        @pl.when(apart(t))
        def _():
            back(0, t).wait_recv()

    for i in range(nx):

        @pl.when(distant(i))
        def _():
            back(i, my_part).wait_send()

    out_ref[...] = result[...]


def slab_scratch(counts, tx, ty, tz, count, steps):
    nx = counts[0]
    own = ty // nx
    rows = own + 2 * DEEP
    full_x = tx * nx
    sem = pltpu.SemaphoreType.DMA
    return [
        pltpu.VMEM((3, full_x, rows, 2 * tz), jnp.float32),
        pltpu.VMEM((3, tx, ty, tz), jnp.float32),
        pltpu.VMEM((2, 2, 3, full_x, DEEP, tz), jnp.float32),
        pltpu.VMEM((2, 2, 3, rows, tz), jnp.float32),
        pltpu.VMEM((2, 3, own, tz), jnp.float32),
        pltpu.VMEM((full_x, rows, tz), jnp.float32),
        pltpu.VMEM((nx, steps, count), jnp.bfloat16),
        pltpu.VMEM((nx, 1, count), jnp.int32),
        pltpu.VMEM((nx, 1, count), jnp.int32),
        pltpu.VMEM((tx, ty, tz), jnp.float32),
        sem((8, 3)),
        sem((8, 3)),
        sem((nx, 2)),
        sem((nx, 2)),
        sem((nx, 3)),
        sem((nx, 3)),
        sem((nx,)),
        sem((nx,)),
        pltpu.VMEM((tx // 2, ty // 2), jnp.int32),
        pltpu.VMEM((tx // 2, ty // 2), jnp.int32),
        sem((5,)),
    ]


def slabs_fit(counts, tx, ty, tz, steps):
    own = ty // counts[0]
    return (
        own * counts[0] == ty
        and own % DEEP == 0
        and tx * counts[0] * DEEP == tz
        and steps % DEEP == 0
        and steps <= tz
    )


def face_scratch(counts, tx, ty, tz, count, steps):
    others = max(counts[0] - 1, 1)
    return [
        pltpu.VMEM((2, tx, ty, tz), jnp.float32),
        pltpu.VMEM((2, 2, ty, tz), jnp.float32),
        pltpu.VMEM((2, 2, tx, tz), jnp.float32),
        pltpu.VMEM((2, 2, 8, tz), jnp.float32),
        pltpu.VMEM((2, 2, tx, tz), jnp.float32),
        pltpu.VMEM((2, 2, 8, tz), jnp.float32),
        pltpu.VMEM((tx, ty, tz), jnp.float32),
        pltpu.VMEM((tx, ty, tz), jnp.float32),
        pltpu.VMEM((others, steps, count), jnp.bfloat16),
        pltpu.VMEM((others, 2, count), jnp.int32),
        pltpu.SemaphoreType.DMA((6, 2)),
        pltpu.SemaphoreType.DMA((6, 2)),
        pltpu.SemaphoreType.DMA((others, 2)),
        pltpu.SemaphoreType.DMA((others, 2)),
    ]


def local(counts, traces, receiver_cell, weight_class, weight_table, top, thick, courant, now, before):
    tx, ty, tz = courant.shape
    count, steps = traces.shape
    vmem = pl.BlockSpec(memory_space=pltpu.VMEM)
    smem = pl.BlockSpec(memory_space=pltpu.SMEM)
    if slabs_fit(counts, tx, ty, tz, steps):
        body, number, place = slab_kernel, 1, pl.BlockSpec(memory_space=pl.ANY)
        tags = [receiver_cell[None], weight_class[None]]
        scratch = slab_scratch(counts, tx, ty, tz, count, steps)
    else:
        body, number, place = kernel, 0, vmem
        tags = [jnp.stack([receiver_cell, weight_class])]
        scratch = face_scratch(counts, tx, ty, tz, count, steps)
    return pl.pallas_call(
        functools.partial(body, counts, ty * counts[1], steps),
        out_shape=jax.ShapeDtypeStruct((tx, ty, tz), jnp.float32),
        in_specs=[place] * (1 + len(tags)) + [smem] + [place] * 5,
        out_specs=vmem,
        scratch_shapes=scratch,
        compiler_params=pltpu.CompilerParams(
            collective_id=number, has_side_effects=True, vmem_limit_bytes=56 * 1024 * 1024
        ),
    )(traces.T, *tags, weight_table, top, thick, courant, now, before)


def solution(mesh):
    counts = tuple(mesh.shape[a] for a in AXES)
    tile = P("gx", "gy", "gz")
    columns = P("gx", "gy")
    placed = (P("gx", None), P("gx"), P("gx"), P(), columns, columns, tile, tile, tile)
    return jax.shard_map(
        functools.partial(local, counts), mesh=mesh, in_specs=placed, out_specs=tile, check_vma=False
    )
```
